32 devices in a mesh: layer: 4 (over y, x), tx: 2 (over core), ty: 4 (over z).
Axes of the slice: x: 2, y: 2, z: 4, core: 2. Of those that a mesh axis runs over, the one named last changes fastest.
Arguments:
- shunt_conductance: float32 [4, 64, 512], P('layer', 'tx', 'ty'), may hold values from 0.02 to 2
- agg_map: int32 [4, 64, 512], P('layer', 'tx', 'ty'), may hold values from 0 to 127, as said below
- slot_current: float32 [4, 2, 4, 8, 128], P('layer', 'tx', 'ty'), may hold values from -12 to 12
- slot_node: int32 [4, 2, 4, 8, 128], P('layer', 'tx', 'ty'), may hold values from 0 to 4095
- slot_count: int32 [4, 2, 4, 8], P('layer', 'tx', 'ty'), may hold values from 16 to 128, as said below
Outputs:
- voltage_drop: float32 [4, 64, 512], P('layer', 'tx', 'ty')
- residual: float32 [4, 64, 512], P('layer', 'tx', 'ty')
The draws below stay inside these ranges and needn't reach their ends.
Inputs may be any that keep to these rules, and one draw needn't show every extreme that they name: `slot_count`: live slots in each block from one source tile to one destination tile, at least 16; slots past them are padding, and at least one block is full. `agg_map`: coarse cell numbered row-major over the 8 x 16 coarse cells of the node's own die tile.
All inputs are finite; a program needn't handle non-finite values.
Results may differ from the reference program's by a relative error of at most 0.0003.
Values sent between devices are 32-bit elements; how exact they have to be, the bound alone decides.
A program may use at most 64 MiB of HBM per device.

```python
import math
import jax
import jax.numpy as jnp
from jax import lax

CX = 32
CY = 128
CGX = 8
CGY = 16
CAP = 128
ITERS = 3
SWEEPS = 3
LAYERS = 4
NX = 64
NY = 512
TILES = 8
N_TX = 2
N_TY = 4


def draw_agg_map(key, part):
    shape = (LAYERS, NX, NY)
    block_rows = CX // CGX
    block_cols = CY // CGY
    reach_rows = max(1, block_rows // 4)
    reach_cols = max(1, block_cols // 4)
    first_key = jax.random.fold_in(key, 11)
    second_key = jax.random.fold_in(key, 12)
    shift_rows = jax.random.randint(first_key, shape, -reach_rows, reach_rows + 1)
    shift_cols = jax.random.randint(second_key, shape, -reach_cols, reach_cols + 1)
    local_rows = lax.broadcasted_iota(jnp.int32, shape, 1) % CX
    local_cols = lax.broadcasted_iota(jnp.int32, shape, 2) % CY
    coarse_row = jnp.clip((local_rows + shift_rows) // block_rows, 0, CGX - 1)
    coarse_col = jnp.clip((local_cols + shift_cols) // block_cols, 0, CGY - 1)
    return (coarse_row * CGY + coarse_col).astype(jnp.int32)


def draw_slot_count(key, part):
    shape = (LAYERS, NX // CX, NY // CY, TILES)
    first_key = jax.random.fold_in(key, 21)
    second_key = jax.random.fold_in(key, 22)
    heat = jax.random.randint(first_key, (TILES,), 1, 5)
    base = jax.random.randint(second_key, shape, CAP // 8, CAP // 4 + 1)
    counts = jnp.minimum(CAP, base * heat[None, None, None, :])
    return counts.at[0, 0, 0, 0].set(CAP).astype(jnp.int32)


def with_ends(drawn, own_key, low, high):
    longest = drawn.shape.index(max(drawn.shape))
    spots = []
    for shift in (0, 1):
        where = [jax.random.randint(jax.random.fold_in(own_key, axis), (), 0, length) for axis, length in enumerate(drawn.shape)]
        where[longest] = (where[longest] + shift) % drawn.shape[longest]
        spots.append(tuple(where))
    return drawn.at[spots[0]].set(low).at[spots[1]].set(high)


def block_levels(rng, dims, shards, smallest, top_value):
    gain = 1.0
    for position, shards_of in shards:
        steps = jax.random.uniform(jax.random.fold_in(jax.random.fold_in(rng, 6), position), (shards_of,), jnp.float32, smallest / len(shards), top_value / len(shards))
        gain = gain * jnp.repeat(jnp.exp(steps), dims[position] // shards_of).reshape((-1,) + (1,) * (len(dims) - 1 - position))
    return gain


def bell_draw(key, extent, deviation, most, shards=(), held_as=jnp.bfloat16):
    drawn = deviation * jax.random.normal(key, extent, jnp.float32)
    if shards:
        drawn = drawn * block_levels(key, extent, shards, -0.22, 0.18)
    return jnp.clip(drawn, -most, most).astype(held_as)


def setup_inputs(seed: int = 0) -> dict:
    streams_of = jax.random.split(jax.random.key(seed), 6)
    return {
        "shunt_conductance": jnp.clip(jnp.exp(math.log(2.0) - 4.6051702 * jax.random.uniform(streams_of[0], (LAYERS, NX, NY), jnp.float32) ** block_levels(streams_of[0], (LAYERS, NX, NY), ((0, 4), (1, 2), (2, 4)), -0.2, 0.2)), 0.02, 2.0),
        "agg_map": draw_agg_map(jax.random.fold_in(streams_of[5], 71), 0),
        "slot_current": bell_draw(streams_of[2], (LAYERS, N_TX, N_TY, TILES, CAP), 3.0, 12.0, ((0, 4), (1, 2), (2, 4)), jnp.float32),
        "slot_node": with_ends(jax.random.randint(streams_of[3], (LAYERS, N_TX, N_TY, TILES, CAP), 0, CX * CY), jax.random.fold_in(streams_of[3], 1), 0, (CX * CY) - 1).astype(jnp.int32),
        "slot_count": draw_slot_count(jax.random.fold_in(streams_of[5], 71), 0),
    }


VIA_CONDUCTANCE = 0.5
COARSE_EDGE = 8.0
RELAXATION = 0.6


def operate(source_field, diagonal):
    padded = jnp.pad(source_field, 1)
    lateral = padded[1:-1, 2:, 1:-1] + padded[1:-1, :-2, 1:-1] + padded[1:-1, 1:-1, 2:] + padded[1:-1, 1:-1, :-2]
    vertical = padded[2:, 1:-1, 1:-1] + padded[:-2, 1:-1, 1:-1]
    return diagonal * source_field - lateral - VIA_CONDUCTANCE * vertical


def coarse_sweep(potential, coarse_rhs, coarse_diag, padded):
    beside = padded[..., 2:, 1:-1] + padded[..., :-2, 1:-1] + padded[..., 1:-1, 2:] + padded[..., 1:-1, :-2]
    return potential + RELAXATION * (coarse_rhs - (coarse_diag * potential - COARSE_EDGE * beside)) / coarse_diag


def reference(shunt_conductance, agg_map, slot_current, slot_node, slot_count):
    shape = (LAYERS, NX, NY)
    layer_index = lax.broadcasted_iota(jnp.int32, shape, 0)
    row_index = lax.broadcasted_iota(jnp.int32, shape, 1)
    col_index = lax.broadcasted_iota(jnp.int32, shape, 2)
    coarse_rows = N_TX * CGX
    coarse_cols = N_TY * CGY
    grid_row = (row_index // CX) * CGX + agg_map // CGY
    grid_col = (col_index // CY) * CGY + agg_map % CGY
    coarse_ids = ((layer_index * coarse_rows + grid_row) * coarse_cols + grid_col).reshape(-1).astype(jnp.int32)
    coarse_total = LAYERS * coarse_rows * coarse_cols

    def restrict(source_field):
        summed = jax.ops.segment_sum(source_field.reshape(-1), coarse_ids, coarse_total)
        return summed.reshape(LAYERS, coarse_rows, coarse_cols)

    diagonal = shunt_conductance + (4.0 + 2.0 * VIA_CONDUCTANCE)
    coarse_diag = 4.0 * COARSE_EDGE + restrict(shunt_conductance + 2.0 * VIA_CONDUCTANCE)

    def precondition(residual):
        coarse_rhs = restrict(residual)
        potential = RELAXATION * coarse_rhs / coarse_diag
        for sweep_turn in range(SWEEPS - 1):
            padded = jnp.pad(potential, ((0, 0), (1, 1), (1, 1)))
            potential = coarse_sweep(potential, coarse_rhs, coarse_diag, padded)
        return residual / diagonal + potential.reshape(-1)[coarse_ids].reshape(shape)

    slot_shape = slot_current.shape
    live_mask = lax.broadcasted_iota(jnp.int32, slot_shape, 4) < slot_count[..., None]
    currents = jnp.where(live_mask, slot_current, jnp.zeros_like(slot_current))
    slot_layer = lax.broadcasted_iota(jnp.int32, slot_shape, 0)
    dest_tile = lax.broadcasted_iota(jnp.int32, slot_shape, 3)
    dest_row = (dest_tile // N_TY) * CX + slot_node // CY
    dest_col = (dest_tile % N_TY) * CY + slot_node % CY
    node_ids = ((slot_layer * NX + dest_row) * NY + dest_col).reshape(-1).astype(jnp.int32)
    sources = jax.ops.segment_sum(currents.reshape(-1), node_ids, LAYERS * NX * NY).reshape(shape)

    voltage = jnp.zeros_like(sources)
    residual = sources
    smoothed = precondition(residual)
    direction = smoothed
    curv_now = jnp.sum(residual * smoothed)
    for iteration in range(ITERS):
        image = operate(direction, diagonal)
        step_size = curv_now / jnp.sum(direction * image)
        voltage = voltage + step_size * direction
        residual = residual - step_size * image
        smoothed = precondition(residual)
        curv_next = jnp.sum(residual * smoothed)
        direction = smoothed + (curv_next / curv_now) * direction
        curv_now = curv_next
    return voltage, residual
```

```python
import functools

import jax
import jax.numpy as jnp
from jax import lax
from jax.experimental import pallas as pl
from jax.experimental.pallas import tpu as pltpu
from jax.sharding import PartitionSpec as P

CGX = 8
CGY = 16
ITERS = 3
SWEEPS = 3
VIA_CONDUCTANCE = 0.5
COARSE_EDGE = 8.0
RELAXATION = 0.6
SHIFT = 1.25
MESH = pl.DeviceIdType.MESH
AROUND = [(a, b) for a in (-1, 0, 1) for b in (-1, 0, 1)]
SIDES = [(-1, 0, 0), (1, 0, 0), (0, -1, 0), (0, 1, 0), (0, 0, -1), (0, 0, 1)]


def iota(shape, dim):
    return lax.broadcasted_iota(jnp.int32, shape, dim)


def each(count, step):
    if count <= 8:
        for k in range(1, count):
            step(k)
    else:
        def run(k, carry):
            step(k)
            return carry

        lax.fori_loop(1, count, run, 0)


def quadratic(moments, coefs):
    total = 0.0
    for i, a in enumerate(coefs):
        for j, b in enumerate(coefs):
            total = total + a * b * moments[i + j]
    return total


def kernel(
    dims,
    shunt_ref, agg_ref, current_ref, node_ref, count_ref,
    voltage_ref, residual_ref,
    msg, box, row_hot, col_hot, coarse_out, coarse_in, field_out, field_in,
    part_out, part_tile, part_layer,
    msg_s, msg_r, coarse_s, coarse_r, field_s, field_r, tile_s, tile_r, layer_s, layer_r,
):
    layers, n_tx, n_ty = dims
    tiles = n_tx * n_ty
    height, breadth = shunt_ref.shape[1], shunt_ref.shape[2]
    lay = lax.axis_index("layer")
    tx = lax.axis_index("tx")
    ty = lax.axis_index("ty")
    me = tx * n_ty + ty

    def tile_device(d):
        return {"layer": lay, "tx": d // n_ty, "ty": lax.rem(d, n_ty)}

    def layer_device(l):
        return {"layer": l, "tx": tx, "ty": ty}

    def beside_layer(da, dx, dy):
        here = True
        for value, delta, size in ((lay, da, layers), (tx, dx, n_tx), (ty, dy, n_ty)):
            if delta < 0:
                here = jnp.logical_and(here, value > 0)
            if delta > 0:
                here = jnp.logical_and(here, value < size - 1)
        return here

    barrier = pltpu.get_barrier_semaphore()
    each(tiles, lambda k: pl.semaphore_signal(
        barrier, inc=1, device_id=tile_device(lax.rem(me + k, tiles)), device_id_type=MESH))
    each(layers, lambda k: pl.semaphore_signal(
        barrier, inc=1, device_id=layer_device(lax.rem(lay + k, layers)), device_id_type=MESH))

    for k, (a, b) in enumerate(AROUND):
        if (a, b) != (0, 0):
            @pl.when(jnp.logical_not(beside_layer(0, a, b)))
            def _(k=k):
                coarse_in[:, k] = jnp.zeros((ITERS + 1,) + coarse_in.shape[2:], jnp.float32)
    for k, side in enumerate(SIDES):
        @pl.when(jnp.logical_not(beside_layer(*side)))
        def _(k=k):
            field_in[:, k] = jnp.zeros((ITERS,) + field_in.shape[2:], jnp.float32)

    square = (tiles, tiles)
    counts = jnp.broadcast_to(count_ref[0, 0].astype(jnp.float32), square)
    counts = jnp.sum(
        jnp.where(iota(square, 0) == iota(square, 1), counts, 0.0), axis=1, keepdims=True)
    slots = current_ref.shape[3:]
    msg[:, 0, :] = jnp.where(iota(slots, 1).astype(jnp.float32) < counts, current_ref[0, 0, 0], 0.0)
    msg[:, 1, :] = node_ref[0, 0, 0].astype(jnp.float32)

    pl.semaphore_wait(barrier, tiles + layers - 2)

    def slot_copy(k):
        return pltpu.make_async_remote_copy(
            src_ref=msg.at[lax.rem(me + k, tiles)], dst_ref=box.at[me],
            send_sem=msg_s.at[k], recv_sem=msg_r.at[k],
            device_id=tile_device(lax.rem(me + k, tiles)), device_id_type=MESH)

    def slot_arrival(k):
        return pltpu.make_async_remote_copy(
            src_ref=msg.at[me], dst_ref=box.at[lax.rem(me + tiles - k, tiles)],
            send_sem=msg_s.at[k], recv_sem=msg_r.at[k],
            device_id=tile_device(lax.rem(me + k, tiles)), device_id_type=MESH)

    each(tiles, lambda k: slot_copy(k).start())
    box[me] = msg[me]

    agg = agg_ref[0]
    agg_p = agg // CGY
    agg_q = agg % CGY
    for i in range(height):
        hot = agg_p[i:i + 1, :] == iota((CGX, breadth), 0)
        row_hot[i] = jnp.where(hot, 1.0, 0.0)
        hot = agg_q[i:i + 1, :] == iota((CGY, breadth), 0)
        ch, half = i // 2, i % 2
        col_hot[CGY * ch:CGY * (ch + 1), breadth * half:breadth * (half + 1)] = jnp.where(
            hot, 1.0, 0.0).astype(jnp.bfloat16)

    lane = iota((CGX, breadth), 1)
    group = lane // CGY
    shift_sub = pltpu.roll

    def restrict(v):
        high = v.astype(jnp.bfloat16).astype(jnp.float32)
        low = v - high
        rows = []
        for ch in range(height // 2):
            cols = []
            for i in (2 * ch, 2 * ch + 1):
                mask = row_hot[i]
                cols.append(jnp.concatenate(
                    [mask * high[i:i + 1, :], mask * low[i:i + 1, :]], axis=0
                ).astype(jnp.bfloat16))
            rows.append(jnp.concatenate(cols, axis=1))
        left = jnp.concatenate(rows, axis=0)
        full = lax.dot_general(
            left, col_hot[...], (((1,), (1,)), ((), ())), preferred_element_type=jnp.float32)
        total = jnp.zeros((CGX, breadth), jnp.float32)
        for ch in range(height // 2):
            at = breadth * (ch // 8)
            piece = full[16 * ch:16 * ch + 8, at:at + breadth] + full[
                16 * ch + 8:16 * ch + 16, at:at + breadth]
            total = total + jnp.where(group == ch % 8, piece, 0.0)
        for shift in (64, 32, 16):
            total = total + pltpu.roll(total, shift, 1)
        return total

    def coarse_copy(turn, k):
        a, b = AROUND[k]
        return pltpu.make_async_remote_copy(
            src_ref=coarse_out.at[turn], dst_ref=coarse_in.at[turn, 8 - k],
            send_sem=coarse_s.at[turn, k], recv_sem=coarse_r.at[turn, 8 - k],
            device_id={"layer": lay, "tx": tx + a, "ty": ty + b}, device_id_type=MESH)

    def coarse_arrival(turn, k):
        a, b = AROUND[k]
        return pltpu.make_async_remote_copy(
            src_ref=coarse_out.at[turn], dst_ref=coarse_in.at[turn, k],
            send_sem=coarse_s.at[turn, k], recv_sem=coarse_r.at[turn, k],
            device_id={"layer": lay, "tx": tx + a, "ty": ty + b}, device_id_type=MESH)

    def coarse_each(step):
        for k, (a, b) in enumerate(AROUND):
            if (a, b) != (0, 0):
                @pl.when(beside_layer(0, a, b))
                def _(k=k):
                    step(k)

    def coarse_block(turn, own):
        rows = []
        for a in range(3):
            west = coarse_in[turn, 3 * a]
            mid = own if a == 1 else coarse_in[turn, 3 * a + 1]
            east = coarse_in[turn, 3 * a + 2]
            row = jnp.where(group == 0, west, jnp.where(group == 1, mid, east))
            rows.append(jnp.where(group < 3, row, 0.0))
        return jnp.concatenate(rows, axis=0)

    def side_part(k, ref):
        if k == 2:
            return ref.at[0:8]
        if k == 3:
            return ref.at[height - 8:height]
        return ref

    def field_copy(turn, k):
        da, dx, dy = SIDES[k]
        return pltpu.make_async_remote_copy(
            src_ref=side_part(k, field_out.at[turn]),
            dst_ref=side_part(k, field_in.at[turn, k ^ 1]),
            send_sem=field_s.at[turn, k], recv_sem=field_r.at[turn, k ^ 1],
            device_id={"layer": lay + da, "tx": tx + dx, "ty": ty + dy}, device_id_type=MESH)

    def field_arrival(turn, k):
        da, dx, dy = SIDES[k]
        return pltpu.make_async_remote_copy(
            src_ref=side_part(k ^ 1, field_out.at[turn]),
            dst_ref=side_part(k ^ 1, field_in.at[turn, k]),
            send_sem=field_s.at[turn, k], recv_sem=field_r.at[turn, k],
            device_id={"layer": lay + da, "tx": tx + dx, "ty": ty + dy}, device_id_type=MESH)

    def field_each(step):
        for k, side in enumerate(SIDES):
            @pl.when(beside_layer(*side))
            def _(k=k):
                step(k)

    shunt = shunt_ref[0]
    diagonal = shunt + (4.0 + 2.0 * VIA_CONDUCTANCE)
    own_diag = 4.0 * COARSE_EDGE + restrict(shunt + 2.0 * VIA_CONDUCTANCE)
    coarse_out[ITERS] = own_diag
    coarse_each(lambda k: coarse_copy(ITERS, k).start())
    inverse = 1.0 / diagonal

    each(tiles, lambda k: slot_arrival(k).wait_recv())

    def scatter(first):
        lefts, rights = [], []
        for k in range(8):
            amount = box[first + k, 0:1, :]
            node = box[first + k, 1:2, :].astype(jnp.int32)
            row = node // breadth
            col = node % breadth
            hot = iota((height, breadth), 0) == row
            parts = []
            for _ in range(3):
                rounded = amount.astype(jnp.bfloat16).astype(jnp.float32)
                parts.append(jnp.where(hot, rounded, 0.0).astype(jnp.bfloat16))
                amount = amount - rounded
            lefts.append(jnp.concatenate(parts, axis=0))
            hot = iota((breadth, breadth), 0) == col
            rights.append(jnp.where(hot, 1.0, 0.0).astype(jnp.bfloat16))
        full = lax.dot_general(
            jnp.concatenate(lefts, axis=1), jnp.concatenate(rights, axis=1),
            (((1,), (1,)), ((), ())), preferred_element_type=jnp.float32)
        return full[:height] + full[height:2 * height] + full[2 * height:]

    if tiles == 8:
        sources = scatter(0)
    else:
        sources = lax.fori_loop(
            0, tiles // 8, lambda g, total: total + scatter(8 * g),
            jnp.zeros((height, breadth), jnp.float32))

    big = (height, breadth)
    big_lane = iota(big, 1)
    big_row = iota(big, 0)
    power = sources
    powers, smooths = [sources], []
    for turn in range(ITERS):
        own = restrict(power)
        coarse_out[turn] = own
        coarse_each(lambda k: coarse_copy(turn, k).start())
        local = power * inverse
        if turn == 0:
            coarse_each(lambda k: coarse_arrival(ITERS, k).wait_recv())
            coarse_diag = coarse_block(ITERS, own_diag)
            coarse_inverse = jnp.where(
                coarse_diag > 0.0, RELAXATION / jnp.maximum(coarse_diag, 1.0), 0.0)
        coarse_each(lambda k: coarse_arrival(turn, k).wait_recv())
        rhs = coarse_block(turn, own)
        potential = rhs * coarse_inverse
        for sweep in range(SWEEPS - 1):
            beside = (
                pltpu.roll(potential, 1, 1) + pltpu.roll(potential, breadth - 1, 1)
                + pltpu.roll(potential, 1, 0) + pltpu.roll(potential, 3 * CGX - 1, 0))
            potential = potential + coarse_inverse * (
                rhs - (coarse_diag * potential - COARSE_EDGE * beside))
        table = jnp.where(group == 1, potential[CGX:2 * CGX], 0.0)
        for shift in (16, 32, 64):
            table = table + pltpu.roll(table, shift, 1)
        table = jnp.where(group == iota((CGX, breadth), 0), table, 0.0)
        for shift in (4, 2, 1):
            table = table + pltpu.roll(table, shift, 0)
        smooth = local + jnp.concatenate(
            [jnp.take_along_axis(table, agg[8 * i:8 * i + 8], axis=1, mode="promise_in_bounds")
             for i in range(height // 8)], axis=0)
        field_out[turn] = smooth
        field_each(lambda k: field_copy(turn, k).start())
        field_each(lambda k: field_arrival(turn, k).wait_recv())
        north = jnp.where(
            big_row == 0, field_in[turn, 2, height - 1:height, :], pltpu.roll(smooth, 1, 0))
        south = jnp.where(
            big_row == height - 1, field_in[turn, 3, 0:1, :], pltpu.roll(smooth, height - 1, 0))
        west = pltpu.roll(
            jnp.where(big_lane == breadth - 1, field_in[turn, 4], smooth), 1, 1)
        east = pltpu.roll(
            jnp.where(big_lane == 0, field_in[turn, 5], smooth), breadth - 1, 1)
        image = (diagonal * smooth - (north + south + west + east)
                 - VIA_CONDUCTANCE * (field_in[turn, 0] + field_in[turn, 1]))
        power = image - SHIFT * power
        powers.append(power)
        smooths.append(smooth)

    for k in range(2 * ITERS):
        product = powers[(k + 1) // 2] * smooths[k // 2]
        part_out[0, k:k + 1, :] = jnp.sum(product, axis=0, keepdims=True)
    part_out[0, 6:8, :] = jnp.zeros((2, breadth), jnp.float32)

    def tile_copy(k):
        return pltpu.make_async_remote_copy(
            src_ref=part_out.at[0], dst_ref=part_tile.at[me],
            send_sem=tile_s.at[k], recv_sem=tile_r.at[k],
            device_id=tile_device(lax.rem(me + k, tiles)), device_id_type=MESH)

    def tile_arrival(k):
        return pltpu.make_async_remote_copy(
            src_ref=part_out.at[0], dst_ref=part_tile.at[lax.rem(me + tiles - k, tiles)],
            send_sem=tile_s.at[k], recv_sem=tile_r.at[k],
            device_id=tile_device(lax.rem(me + k, tiles)), device_id_type=MESH)

    def layer_copy(k):
        return pltpu.make_async_remote_copy(
            src_ref=part_out.at[1], dst_ref=part_layer.at[lay],
            send_sem=layer_s.at[k], recv_sem=layer_r.at[k],
            device_id=layer_device(lax.rem(lay + k, layers)), device_id_type=MESH)

    def layer_arrival(k):
        return pltpu.make_async_remote_copy(
            src_ref=part_out.at[1], dst_ref=part_layer.at[lax.rem(lay + layers - k, layers)],
            send_sem=layer_s.at[k], recv_sem=layer_r.at[k],
            device_id=layer_device(lax.rem(lay + k, layers)), device_id_type=MESH)

    each(tiles, lambda k: tile_copy(k).start())
    part_tile[me] = part_out[0]
    each(tiles, lambda k: tile_arrival(k).wait_recv())
    part_out[1] = jnp.sum(part_tile[...], axis=0)
    each(layers, lambda k: layer_copy(k).start())
    part_layer[lay] = part_out[1]
    each(layers, lambda k: layer_arrival(k).wait_recv())
    sums = jnp.sum(jnp.sum(part_layer[...], axis=0), axis=1, keepdims=True)
    moments = [sums[k:k + 1, :] for k in range(2 * ITERS)]
    energies = [moments[k + 1] + SHIFT * moments[k] for k in range(2 * ITERS - 1)]

    res, way, volt = [1.0], [1.0], []
    curv = moments[0]
    for turn in range(ITERS):
        step = curv / quadratic(energies, way)
        volt = [(volt[i] if i < len(volt) else 0.0) + step * way[i] for i in range(turn + 1)]
        image = [0.0] * (turn + 2)
        for i in range(turn + 1):
            image[i + 1] = image[i + 1] + way[i]
            image[i] = image[i] + SHIFT * way[i]
        res = [(res[i] if i < len(res) else 0.0) - step * image[i] for i in range(turn + 2)]
        if turn + 1 < ITERS:
            newer = quadratic(moments, res)
            ratio = newer / curv
            way = [res[i] + (ratio * way[i] if i < len(way) else 0.0) for i in range(turn + 2)]
            curv = newer
    voltage = volt[0] * smooths[0]
    residual = res[0] * powers[0]
    for i in range(1, ITERS):
        voltage = voltage + volt[i] * smooths[i]
    for i in range(1, ITERS + 1):
        residual = residual + res[i] * powers[i]
    voltage_ref[0] = voltage
    residual_ref[0] = residual

    each(tiles, lambda k: slot_copy(k).wait_send())
    for turn in range(ITERS + 1):
        coarse_each(lambda k: coarse_copy(turn, k).wait_send())
    for turn in range(ITERS):
        field_each(lambda k: field_copy(turn, k).wait_send())
    each(tiles, lambda k: tile_copy(k).wait_send())
    each(layers, lambda k: layer_copy(k).wait_send())


def solution(mesh):
    layers, n_tx, n_ty = mesh.shape["layer"], mesh.shape["tx"], mesh.shape["ty"]
    tiles = n_tx * n_ty

    def body(shunt, agg, current, node, count):
        height, breadth = shunt.shape[1], shunt.shape[2]
        f32 = jnp.float32
        dma = pltpu.SemaphoreType.DMA
        vmem = pl.BlockSpec(memory_space=pltpu.VMEM)
        return tuple(pl.pallas_call(
            functools.partial(kernel, (layers, n_tx, n_ty)),
            out_shape=[jax.ShapeDtypeStruct(shunt.shape, f32)] * 2,
            in_specs=[vmem] * 5,
            out_specs=[vmem] * 2,
            scratch_shapes=[
                pltpu.VMEM((tiles, 2, current.shape[4]), f32),
                pltpu.VMEM((tiles, 2, current.shape[4]), f32),
                pltpu.VMEM((height, CGX, breadth), f32),
                pltpu.VMEM((CGY * height // 2, 2 * breadth), jnp.bfloat16),
                pltpu.VMEM((ITERS + 1, CGX, breadth), f32),
                pltpu.VMEM((ITERS + 1, 9, CGX, breadth), f32),
                pltpu.VMEM((ITERS, height, breadth), f32),
                pltpu.VMEM((ITERS, 6, height, breadth), f32),
                pltpu.VMEM((2, 8, breadth), f32),
                pltpu.VMEM((tiles, 8, breadth), f32),
                pltpu.VMEM((layers, 8, breadth), f32),
                dma((tiles,)), dma((tiles,)),
                dma((ITERS + 1, 9)), dma((ITERS + 1, 9)),
                dma((ITERS, 6)), dma((ITERS, 6)),
                dma((tiles,)), dma((tiles,)),
                dma((layers,)), dma((layers,)),
            ],
            compiler_params=pltpu.CompilerParams(
                collective_id=0, has_side_effects=True, vmem_limit_bytes=32 * 1024 * 1024),
        )(shunt, agg, current, node, count))

    in_specs = (
        P("layer", "tx", "ty"),
        P("layer", "tx", "ty"),
        P("layer", "tx", "ty", None, None),
        P("layer", "tx", "ty", None, None),
        P("layer", "tx", "ty", None),
    )
    out_specs = (P("layer", "tx", "ty"), P("layer", "tx", "ty"))

    def run(*args):
        voltage, residual = jax.shard_map(
            body, mesh=mesh, in_specs=in_specs, out_specs=out_specs, check_vma=False)(*args)
        return voltage, residual

    return run
```

```python
import functools

import jax
import jax.numpy as jnp
from jax import lax
from jax.experimental import pallas as pl
from jax.experimental.pallas import tpu as pltpu
from jax.sharding import PartitionSpec as P

CGX = 8
CGY = 16
ITERS = 3
SWEEPS = 3
VIA_CONDUCTANCE = 0.5
COARSE_EDGE = 8.0
RELAXATION = 0.6
SHIFT = 1.25
MESH = pl.DeviceIdType.MESH
AROUND = [(a, b) for a in (-1, 0, 1) for b in (-1, 0, 1)]
SIDES = [(-1, 0, 0), (1, 0, 0), (0, -1, 0), (0, 1, 0), (0, 0, -1), (0, 0, 1)]


def iota(shape, dim):
    return lax.broadcasted_iota(jnp.int32, shape, dim)


def each(count, step):
    if count <= 32:
        for k in range(1, count):
            step(k)
    else:
        def run(k, carry):
            step(k)
            return carry

        lax.fori_loop(1, count, run, 0)


def quadratic(moments, coefs):
    total = 0.0
    for i, a in enumerate(coefs):
        for j, b in enumerate(coefs):
            total = total + a * b * moments[i + j]
    return total


def kernel(
    dims,
    shunt_in, agg_in, current_in, node_in, count_in,
    result_ref,
    shunt_ref, agg_ref, current_ref, node_ref, count_ref, input_s,
    msg, box, row_hot, col_hot, coarse_out, coarse_in, field_out, field_in,
    part_out, part_in,
    msg_s, msg_r, coarse_s, coarse_r, field_s, field_r, part_s, part_r,
):
    layers, n_tx, n_ty = dims
    tiles = n_tx * n_ty
    height, breadth = shunt_ref.shape[1], shunt_ref.shape[2]
    lay = lax.axis_index("layer")
    tx = lax.axis_index("tx")
    ty = lax.axis_index("ty")
    me = tx * n_ty + ty

    def tile_device(d):
        return {"layer": lay, "tx": d // n_ty, "ty": lax.rem(d, n_ty)}

    everyone = layers * tiles
    place = lay * tiles + me

    def any_device(d):
        rest = lax.rem(d, tiles)
        return {"layer": d // tiles, "tx": rest // n_ty, "ty": lax.rem(rest, n_ty)}

    loads = [
        pltpu.make_async_copy(source, target, input_s.at[k])
        for k, (source, target) in enumerate((
            (count_in, count_ref), (current_in, current_ref), (node_in, node_ref),
            (agg_in, agg_ref), (shunt_in, shunt_ref)))
    ]
    for load in loads:
        load.start()

    def beside_layer(da, dx, dy):
        here = True
        for value, delta, size in ((lay, da, layers), (tx, dx, n_tx), (ty, dy, n_ty)):
            if delta < 0:
                here = jnp.logical_and(here, value > 0)
            if delta > 0:
                here = jnp.logical_and(here, value < size - 1)
        return here

    barrier = pltpu.get_barrier_semaphore()
    each(everyone, lambda k: pl.semaphore_signal(
        barrier, inc=1, device_id=any_device(lax.rem(place + k, everyone)), device_id_type=MESH))

    for k, (a, b) in enumerate(AROUND):
        if (a, b) != (0, 0):
            @pl.when(jnp.logical_not(beside_layer(0, a, b)))
            def _(k=k):
                coarse_in[:, k] = jnp.zeros((ITERS + 1,) + coarse_in.shape[2:], jnp.float32)
    for k, side in enumerate(SIDES):
        @pl.when(jnp.logical_not(beside_layer(*side)))
        def _(k=k):
            field_in[:, k] = jnp.zeros((ITERS,) + field_in.shape[2:], jnp.float32)

    for load in loads[:3]:
        load.wait()
    square = (tiles, tiles)
    counts = jnp.broadcast_to(count_ref[0, 0].astype(jnp.float32), square)
    counts = jnp.sum(
        jnp.where(iota(square, 0) == iota(square, 1), counts, 0.0), axis=1, keepdims=True)
    slots = current_ref.shape[3:]
    msg[:, 0, :] = jnp.where(iota(slots, 1).astype(jnp.float32) < counts, current_ref[0, 0, 0], 0.0)
    msg[:, 1, :] = node_ref[0, 0, 0].astype(jnp.float32)

    for load in loads[3:]:
        load.wait()
    agg = agg_ref[0]
    agg_p = agg // CGY
    agg_q = agg % CGY
    for i in range(height):
        hot = agg_p[i:i + 1, :] == iota((CGX, breadth), 0)
        row_hot[i] = jnp.where(hot, 1.0, 0.0)
        hot = agg_q[i:i + 1, :] == iota((CGY, breadth), 0)
        ch, half = i // 2, i % 2
        col_hot[CGY * ch:CGY * (ch + 1), breadth * half:breadth * (half + 1)] = jnp.where(
            hot, 1.0, 0.0).astype(jnp.bfloat16)

    lane = iota((CGX, breadth), 1)
    group = lane // CGY
    shift_sub = pltpu.roll

    def restrict(v):
        high = v.astype(jnp.bfloat16).astype(jnp.float32)
        low = v - high
        rows = []
        for ch in range(height // 2):
            cols = []
            for i in (2 * ch, 2 * ch + 1):
                mask = row_hot[i]
                cols.append(jnp.concatenate(
                    [mask * high[i:i + 1, :], mask * low[i:i + 1, :]], axis=0
                ).astype(jnp.bfloat16))
            rows.append(jnp.concatenate(cols, axis=1))
        left = jnp.concatenate(rows, axis=0)
        full = lax.dot_general(
            left, col_hot[...], (((1,), (1,)), ((), ())), preferred_element_type=jnp.float32)
        total = jnp.zeros((CGX, breadth), jnp.float32)
        for ch in range(height // 2):
            at = breadth * (ch // 8)
            piece = full[16 * ch:16 * ch + 8, at:at + breadth] + full[
                16 * ch + 8:16 * ch + 16, at:at + breadth]
            total = total + jnp.where(group == ch % 8, piece, 0.0)
        for shift in (64, 32, 16):
            total = total + pltpu.roll(total, shift, 1)
        return total

    def coarse_copy(turn, k):
        a, b = AROUND[k]
        return pltpu.make_async_remote_copy(
            src_ref=coarse_out.at[turn], dst_ref=coarse_in.at[turn, 8 - k],
            send_sem=coarse_s.at[turn, k], recv_sem=coarse_r.at[turn, 8 - k],
            device_id={"layer": lay, "tx": tx + a, "ty": ty + b}, device_id_type=MESH)

    def coarse_arrival(turn, k):
        a, b = AROUND[k]
        return pltpu.make_async_remote_copy(
            src_ref=coarse_out.at[turn], dst_ref=coarse_in.at[turn, k],
            send_sem=coarse_s.at[turn, k], recv_sem=coarse_r.at[turn, k],
            device_id={"layer": lay, "tx": tx + a, "ty": ty + b}, device_id_type=MESH)

    def coarse_each(step):
        for k, (a, b) in enumerate(AROUND):
            if (a, b) != (0, 0):
                @pl.when(beside_layer(0, a, b))
                def _(k=k):
                    step(k)

    def coarse_block(turn, own):
        rows = []
        for a in range(3):
            west = coarse_in[turn, 3 * a]
            mid = own if a == 1 else coarse_in[turn, 3 * a + 1]
            east = coarse_in[turn, 3 * a + 2]
            row = jnp.where(group == 0, west, jnp.where(group == 1, mid, east))
            rows.append(jnp.where(group < 3, row, 0.0))
        return jnp.concatenate(rows, axis=0)

    def side_part(k, ref):
        if k == 2:
            return ref.at[0:8]
        if k == 3:
            return ref.at[height - 8:height]
        return ref

    def field_copy(turn, k):
        da, dx, dy = SIDES[k]
        return pltpu.make_async_remote_copy(
            src_ref=side_part(k, field_out.at[turn]),
            dst_ref=side_part(k, field_in.at[turn, k ^ 1]),
            send_sem=field_s.at[turn, k], recv_sem=field_r.at[turn, k ^ 1],
            device_id={"layer": lay + da, "tx": tx + dx, "ty": ty + dy}, device_id_type=MESH)

    def field_arrival(turn, k):
        da, dx, dy = SIDES[k]
        return pltpu.make_async_remote_copy(
            src_ref=side_part(k ^ 1, field_out.at[turn]),
            dst_ref=side_part(k ^ 1, field_in.at[turn, k]),
            send_sem=field_s.at[turn, k], recv_sem=field_r.at[turn, k],
            device_id={"layer": lay + da, "tx": tx + dx, "ty": ty + dy}, device_id_type=MESH)

    def field_each(step):
        for k, side in enumerate(SIDES):
            @pl.when(beside_layer(*side))
            def _(k=k):
                step(k)

    shunt = shunt_ref[0]
    diagonal = shunt + (4.0 + 2.0 * VIA_CONDUCTANCE)
    own_diag = 4.0 * COARSE_EDGE + restrict(shunt + 2.0 * VIA_CONDUCTANCE)
    coarse_out[ITERS] = own_diag
    inverse = 1.0 / diagonal

    pl.semaphore_wait(barrier, everyone - 1)

    def slot_copy(k):
        return pltpu.make_async_remote_copy(
            src_ref=msg.at[lax.rem(me + k, tiles)], dst_ref=box.at[me],
            send_sem=msg_s, recv_sem=msg_r,
            device_id=tile_device(lax.rem(me + k, tiles)), device_id_type=MESH)

    def slot_all():
        return pltpu.make_async_remote_copy(
            src_ref=msg.at[pl.ds(0, tiles - 1)], dst_ref=box.at[pl.ds(0, tiles - 1)],
            send_sem=msg_s, recv_sem=msg_r,
            device_id=tile_device(lax.rem(me + 1, tiles)), device_id_type=MESH)

    each(tiles, lambda k: slot_copy(k).start())
    box[me] = msg[me]
    coarse_each(lambda k: coarse_copy(ITERS, k).start())

    slot_all().wait_recv()

    def scatter(first):
        lefts, rights = [], []
        for k in range(8):
            amount = box[first + k, 0:1, :]
            node = box[first + k, 1:2, :].astype(jnp.int32)
            row = node // breadth
            col = node % breadth
            hot = iota((height, breadth), 0) == row
            parts = []
            for _ in range(3):
                rounded = amount.astype(jnp.bfloat16).astype(jnp.float32)
                parts.append(jnp.where(hot, rounded, 0.0).astype(jnp.bfloat16))
                amount = amount - rounded
            lefts.append(jnp.concatenate(parts, axis=0))
            hot = iota((breadth, breadth), 0) == col
            rights.append(jnp.where(hot, 1.0, 0.0).astype(jnp.bfloat16))
        full = lax.dot_general(
            jnp.concatenate(lefts, axis=1), jnp.concatenate(rights, axis=1),
            (((1,), (1,)), ((), ())), preferred_element_type=jnp.float32)
        return full[:height] + full[height:2 * height] + full[2 * height:]

    if tiles == 8:
        sources = scatter(0)
    else:
        sources = lax.fori_loop(
            0, tiles // 8, lambda g, total: total + scatter(8 * g),
            jnp.zeros((height, breadth), jnp.float32))

    big = (height, breadth)
    big_lane = iota(big, 1)
    big_row = iota(big, 0)
    power = sources
    powers, smooths = [sources], []
    for turn in range(ITERS):
        own = restrict(power)
        coarse_out[turn] = own
        coarse_each(lambda k: coarse_copy(turn, k).start())
        local = power * inverse
        if turn == 0:
            slot_all().wait_send()
            coarse_each(lambda k: coarse_copy(ITERS, k).wait_send())
            coarse_each(lambda k: coarse_arrival(ITERS, k).wait_recv())
            coarse_diag = coarse_block(ITERS, own_diag)
            coarse_inverse = jnp.where(
                coarse_diag > 0.0, RELAXATION / jnp.maximum(coarse_diag, 1.0), 0.0)
        else:
            field_each(lambda k: field_copy(turn - 1, k).wait_send())
        coarse_each(lambda k: coarse_arrival(turn, k).wait_recv())
        rhs = coarse_block(turn, own)
        potential = rhs * coarse_inverse
        for sweep in range(SWEEPS - 1):
            beside = (
                pltpu.roll(potential, 1, 1) + pltpu.roll(potential, breadth - 1, 1)
                + pltpu.roll(potential, 1, 0) + pltpu.roll(potential, 3 * CGX - 1, 0))
            potential = potential + coarse_inverse * (
                rhs - (coarse_diag * potential - COARSE_EDGE * beside))
        table = jnp.where(group == 1, potential[CGX:2 * CGX], 0.0)
        for shift in (16, 32, 64):
            table = table + pltpu.roll(table, shift, 1)
        table = jnp.where(group == iota((CGX, breadth), 0), table, 0.0)
        for shift in (4, 2, 1):
            table = table + pltpu.roll(table, shift, 0)
        smooth = local + jnp.concatenate(
            [jnp.take_along_axis(table, agg[8 * i:8 * i + 8], axis=1, mode="promise_in_bounds")
             for i in range(height // 8)], axis=0)
        field_out[turn] = smooth
        field_each(lambda k: field_copy(turn, k).start())
        if turn + 1 < ITERS:
            coarse_each(lambda k: coarse_copy(turn, k).wait_send())
        field_each(lambda k: field_arrival(turn, k).wait_recv())
        north = jnp.where(
            big_row == 0, field_in[turn, 2, height - 1:height, :], pltpu.roll(smooth, 1, 0))
        south = jnp.where(
            big_row == height - 1, field_in[turn, 3, 0:1, :], pltpu.roll(smooth, height - 1, 0))
        west = pltpu.roll(
            jnp.where(big_lane == breadth - 1, field_in[turn, 4], smooth), 1, 1)
        east = pltpu.roll(
            jnp.where(big_lane == 0, field_in[turn, 5], smooth), breadth - 1, 1)
        image = (diagonal * smooth - (north + south + west + east)
                 - VIA_CONDUCTANCE * (field_in[turn, 0] + field_in[turn, 1]))
        power = image - SHIFT * power
        powers.append(power)
        smooths.append(smooth)

    sums = [
        jnp.sum(powers[(k + 1) // 2] * smooths[k // 2], axis=0, keepdims=True)
        for k in range(2 * ITERS)
    ]
    sums.append(jnp.zeros((8 - 2 * ITERS, breadth), jnp.float32))
    sums = jnp.sum(jnp.concatenate(sums, axis=0), axis=1, keepdims=True)
    spot = iota((8, breadth), 0) == lane
    part_out[...] = jnp.sum(jnp.where(spot, sums, 0.0), axis=0, keepdims=True)

    def part_copy(k):
        return pltpu.make_async_remote_copy(
            src_ref=part_out, dst_ref=part_in.at[place], send_sem=part_s, recv_sem=part_r,
            device_id=any_device(lax.rem(place + k, everyone)), device_id_type=MESH)

    def part_all():
        rows = part_in.at[pl.ds(0, everyone - 1)]
        return pltpu.make_async_remote_copy(
            src_ref=rows, dst_ref=rows, send_sem=part_s, recv_sem=part_r,
            device_id=any_device(lax.rem(place + 1, everyone)), device_id_type=MESH)

    each(everyone, lambda k: part_copy(k).start())
    part_in[place] = part_out[...]
    coarse_each(lambda k: coarse_copy(ITERS - 1, k).wait_send())
    field_each(lambda k: field_copy(ITERS - 1, k).wait_send())
    part_all().wait_recv()
    sums = jnp.sum(part_in[...], axis=0)
    sums = jnp.sum(jnp.where(spot, sums, 0.0), axis=1, keepdims=True)
    moments = [sums[k:k + 1, :] for k in range(2 * ITERS)]
    energies = [moments[k + 1] + SHIFT * moments[k] for k in range(2 * ITERS - 1)]

    res, way, volt = [1.0], [1.0], []
    curv = moments[0]
    for turn in range(ITERS):
        step = curv / quadratic(energies, way)
        volt = [(volt[i] if i < len(volt) else 0.0) + step * way[i] for i in range(turn + 1)]
        image = [0.0] * (turn + 2)
        for i in range(turn + 1):
            image[i + 1] = image[i + 1] + way[i]
            image[i] = image[i] + SHIFT * way[i]
        res = [(res[i] if i < len(res) else 0.0) - step * image[i] for i in range(turn + 2)]
        if turn + 1 < ITERS:
            newer = quadratic(moments, res)
            ratio = newer / curv
            way = [res[i] + (ratio * way[i] if i < len(way) else 0.0) for i in range(turn + 2)]
            curv = newer
    voltage = volt[0] * smooths[0]
    residual = res[0] * powers[0]
    for i in range(1, ITERS):
        voltage = voltage + volt[i] * smooths[i]
    for i in range(1, ITERS + 1):
        residual = residual + res[i] * powers[i]
    result_ref[0] = voltage
    result_ref[1] = residual
    part_all().wait_send()


def solution(mesh):
    layers, n_tx, n_ty = mesh.shape["layer"], mesh.shape["tx"], mesh.shape["ty"]
    tiles = n_tx * n_ty

    def body(shunt, agg, current, node, count):
        height, breadth = shunt.shape[1], shunt.shape[2]
        f32 = jnp.float32
        dma = pltpu.SemaphoreType.DMA
        vmem = pl.BlockSpec(memory_space=pltpu.VMEM)
        out = pl.pallas_call(
            functools.partial(kernel, (layers, n_tx, n_ty)),
            out_shape=jax.ShapeDtypeStruct((2,) + shunt.shape[1:], f32),
            in_specs=[pl.BlockSpec(memory_space=pltpu.HBM)] * 5,
            out_specs=vmem,
            scratch_shapes=[
                *(pltpu.VMEM(x.shape, x.dtype) for x in (shunt, agg, current, node, count)),
                dma((5,)),
                pltpu.VMEM((tiles, 2, current.shape[4]), f32),
                pltpu.VMEM((tiles, 2, current.shape[4]), f32),
                pltpu.VMEM((height, CGX, breadth), f32),
                pltpu.VMEM((CGY * height // 2, 2 * breadth), jnp.bfloat16),
                pltpu.VMEM((ITERS + 1, CGX, breadth), f32),
                pltpu.VMEM((ITERS + 1, 9, CGX, breadth), f32),
                pltpu.VMEM((ITERS, height, breadth), f32),
                pltpu.VMEM((ITERS, 6, height, breadth), f32),
                pltpu.VMEM((1, breadth), f32),
                pltpu.VMEM((layers * tiles, 1, breadth), f32),
                dma, dma,
                dma((ITERS + 1, 9)), dma((ITERS + 1, 9)),
                dma((ITERS, 6)), dma((ITERS, 6)),
                dma, dma,
            ],
            compiler_params=pltpu.CompilerParams(
                collective_id=0, has_side_effects=True, vmem_limit_bytes=60 * 1024 * 1024),
        )(shunt, agg, current, node, count)
        return out[0:1], out[1:2]

    in_specs = (
        P("layer", "tx", "ty"),
        P("layer", "tx", "ty"),
        P("layer", "tx", "ty", None, None),
        P("layer", "tx", "ty", None, None),
        P("layer", "tx", "ty", None),
    )
    out_specs = (P("layer", "tx", "ty"), P("layer", "tx", "ty"))

    def run(*args):
        voltage, residual = jax.shard_map(
            body, mesh=mesh, in_specs=in_specs, out_specs=out_specs, check_vma=False)(*args)
        return voltage, residual

    return run
```

```python
import functools

import jax
import jax.numpy as jnp
from jax import lax
from jax.experimental import pallas as pl
from jax.experimental.pallas import tpu as pltpu
from jax.sharding import PartitionSpec as P

CGX = 8
CGY = 16
ITERS = 3
SWEEPS = 3
VIA_CONDUCTANCE = 0.5
COARSE_EDGE = 8.0
RELAXATION = 0.6
SHIFT = 1.25
MESH = pl.DeviceIdType.MESH
SIDES = [(-1, 0, 0), (1, 0, 0), (0, -1, 0), (0, 1, 0), (0, 0, -1), (0, 0, 1)]


def iota(shape, dim):
    return lax.broadcasted_iota(jnp.int32, shape, dim)


def each(count, step):
    if count <= 32:
        for k in range(1, count):
            step(k)
    else:
        def run(k, carry):
            step(k)
            return carry

        lax.fori_loop(1, count, run, 0)


def coarse_places(n_tx, n_ty):
    own = [(0, a, b) for a in range(-2, 3) for b in range(-2, 3)
           if (a, b) != (0, 0) and abs(a) + abs(b) < 4]
    other = [(d, a, b) for d in (-1, 1) for a in (-1, 0, 1) for b in (-1, 0, 1)]
    return [p for p in own + other if abs(p[1]) < n_tx and abs(p[2]) < n_ty]


def quadratic(moments, coefs):
    total = 0.0
    for i, a in enumerate(coefs):
        for j, b in enumerate(coefs):
            total = total + a * b * moments[i + j]
    return total


def kernel(
    dims,
    shunt_in, agg_in, current_in, node_in, count_in,
    result_ref,
    shunt_ref, agg_ref, current_ref, node_ref, count_ref, input_s,
    msg, box, agg_side, row_hot, col_hot, coarse_out, coarse_in, field_out, field_in,
    part_out, part_in,
    msg_s, msg_r, side_s, side_r, coarse_s, coarse_r, field_s, field_r, part_s, part_r,
):
    layers, n_tx, n_ty = dims
    tiles = n_tx * n_ty
    height, breadth = shunt_ref.shape[1], shunt_ref.shape[2]
    lay = lax.axis_index("layer")
    tx = lax.axis_index("tx")
    ty = lax.axis_index("ty")
    me = tx * n_ty + ty
    places = coarse_places(n_tx, n_ty)

    def tile_device(d):
        return {"layer": lay, "tx": d // n_ty, "ty": lax.rem(d, n_ty)}

    everyone = layers * tiles
    place = lay * tiles + me

    def any_device(d):
        rest = lax.rem(d, tiles)
        return {"layer": d // tiles, "tx": rest // n_ty, "ty": lax.rem(rest, n_ty)}

    loads = [
        pltpu.make_async_copy(source, target, input_s.at[k])
        for k, (source, target) in enumerate((
            (count_in, count_ref), (current_in, current_ref), (node_in, node_ref),
            (agg_in, agg_ref), (shunt_in, shunt_ref)))
    ]
    for load in loads:
        load.start()

    def beside_layer(da, dx, dy):
        here = True
        for value, delta, size in ((lay, da, layers), (tx, dx, n_tx), (ty, dy, n_ty)):
            if delta < 0:
                here = jnp.logical_and(here, value >= -delta)
            if delta > 0:
                here = jnp.logical_and(here, value < size - delta)
        return here

    barrier = pltpu.get_barrier_semaphore()
    each(everyone, lambda k: pl.semaphore_signal(
        barrier, inc=1, device_id=any_device(lax.rem(place + k, everyone)), device_id_type=MESH))

    for k, offset in enumerate(places):
        @pl.when(jnp.logical_not(beside_layer(*offset)))
        def _(k=k):
            coarse_in[:, k] = jnp.zeros((ITERS + 1, 1, breadth), jnp.float32)
    for k, side in enumerate(SIDES):
        @pl.when(jnp.logical_not(beside_layer(*side)))
        def _(k=k):
            field_in[:, k] = jnp.zeros((ITERS, height, breadth), jnp.float32)
            agg_side[k] = jnp.zeros((height, breadth), jnp.int32)

    for load in loads[:3]:
        load.wait()
    square = (tiles, tiles)
    counts = jnp.broadcast_to(count_ref[0, 0].astype(jnp.float32), square)
    counts = jnp.sum(
        jnp.where(iota(square, 0) == iota(square, 1), counts, 0.0), axis=1, keepdims=True)
    slots = current_ref.shape[3:]
    msg[:, 0, :] = jnp.where(iota(slots, 1).astype(jnp.float32) < counts, current_ref[0, 0, 0], 0.0)
    msg[:, 1, :] = node_ref[0, 0, 0].astype(jnp.float32)

    for load in loads[3:]:
        load.wait()
    agg = agg_ref[0]
    agg_p = agg // CGY
    agg_q = agg % CGY
    for i in range(height):
        hot = agg_p[i:i + 1, :] == iota((CGX, breadth), 0)
        row_hot[i] = jnp.where(hot, 1.0, 0.0)
        hot = agg_q[i:i + 1, :] == iota((CGY, breadth), 0)
        ch, half = i // 2, i % 2
        col_hot[CGY * ch:CGY * (ch + 1), breadth * half:breadth * (half + 1)] = jnp.where(
            hot, 1.0, 0.0).astype(jnp.bfloat16)

    lane = iota((CGX, breadth), 1)
    group = lane // CGY
    shift_sub = pltpu.roll

    def restrict(v):
        high = v.astype(jnp.bfloat16).astype(jnp.float32)
        low = v - high
        rows = []
        for ch in range(height // 2):
            cols = []
            for i in (2 * ch, 2 * ch + 1):
                mask = row_hot[i]
                cols.append(jnp.concatenate(
                    [mask * high[i:i + 1, :], mask * low[i:i + 1, :]], axis=0
                ).astype(jnp.bfloat16))
            rows.append(jnp.concatenate(cols, axis=1))
        left = jnp.concatenate(rows, axis=0)
        full = lax.dot_general(
            left, col_hot[...], (((1,), (1,)), ((), ())), preferred_element_type=jnp.float32)
        total = jnp.zeros((CGX, breadth), jnp.float32)
        for ch in range(height // 2):
            at = breadth * (ch // 8)
            piece = full[16 * ch:16 * ch + 8, at:at + breadth] + full[
                16 * ch + 8:16 * ch + 16, at:at + breadth]
            total = total + jnp.where(group == ch % 8, piece, 0.0)
        for shift in (64, 32, 16):
            total = total + pltpu.roll(total, shift, 1)
        return total

    cell = CGY * iota((CGX, breadth), 0) + lane % CGY

    def flatten(block):
        block = jnp.where(group == iota((CGX, breadth), 0), block, 0.0)
        return jnp.sum(block, axis=0, keepdims=True)

    def pick(row, index):
        row = jnp.broadcast_to(row, (CGX, breadth))
        return jnp.take_along_axis(row, index, axis=1, mode="promise_in_bounds")

    def coarse_copy(turn, k):
        da, dx, dy = places[k]
        there = places.index((-da, -dx, -dy))
        return pltpu.make_async_remote_copy(
            src_ref=coarse_out.at[turn], dst_ref=coarse_in.at[turn, there],
            send_sem=coarse_s.at[turn, k], recv_sem=coarse_r.at[turn, there],
            device_id={"layer": lay + da, "tx": tx + dx, "ty": ty + dy}, device_id_type=MESH)

    def coarse_arrival(turn, k):
        da, dx, dy = places[k]
        return pltpu.make_async_remote_copy(
            src_ref=coarse_out.at[turn], dst_ref=coarse_in.at[turn, k],
            send_sem=coarse_s.at[turn, k], recv_sem=coarse_r.at[turn, k],
            device_id={"layer": lay + da, "tx": tx + dx, "ty": ty + dy}, device_id_type=MESH)

    def coarse_each(step):
        for k, offset in enumerate(places):
            @pl.when(beside_layer(*offset))
            def _(k=k):
                step(k)

    reach = min(2, n_tx - 1)

    def coarse_blocks(turn, own):
        zero = jnp.zeros((CGX, breadth), jnp.float32)

        def tile(offset):
            if offset == (0, 0, 0):
                return own
            if offset not in places:
                return zero
            return pick(coarse_in[turn, places.index(offset)], cell)

        def line(offsets):
            row = zero
            for g, offset in enumerate(offsets):
                row = jnp.where(group == g, tile(offset), row)
            return row

        same = [line([(0, a, b) for b in range(-2, 3)]) for a in range(-reach, reach + 1)]
        other = [line([(d, a, b) for d in (-1, 1) for b in (-1, 0, 1)]) for a in (-1, 0, 1)]
        return jnp.concatenate(same, axis=0), jnp.concatenate(other, axis=0)

    def sweeps(rhs, diag, inv):
        potential = rhs * inv
        for sweep in range(SWEEPS - 1):
            beside = (
                pltpu.roll(potential, 1, 1) + pltpu.roll(potential, breadth - 1, 1)
                + pltpu.roll(potential, 1, 0) + pltpu.roll(potential, rhs.shape[0] - 1, 0))
            potential = potential + inv * (rhs - (diag * potential - COARSE_EDGE * beside))
        return potential

    def side_part(k, ref):
        if k == 2:
            return ref.at[0:8]
        if k == 3:
            return ref.at[height - 8:height]
        return ref

    def field_copy(turn, k):
        da, dx, dy = SIDES[k]
        return pltpu.make_async_remote_copy(
            src_ref=side_part(k, field_out.at[turn]),
            dst_ref=side_part(k, field_in.at[turn, k ^ 1]),
            send_sem=field_s.at[turn, k], recv_sem=field_r.at[turn, k ^ 1],
            device_id={"layer": lay + da, "tx": tx + dx, "ty": ty + dy}, device_id_type=MESH)

    def field_arrival(turn, k):
        da, dx, dy = SIDES[k]
        return pltpu.make_async_remote_copy(
            src_ref=side_part(k ^ 1, field_out.at[turn]),
            dst_ref=side_part(k ^ 1, field_in.at[turn, k]),
            send_sem=field_s.at[turn, k], recv_sem=field_r.at[turn, k],
            device_id={"layer": lay + da, "tx": tx + dx, "ty": ty + dy}, device_id_type=MESH)

    def side_copy(k):
        da, dx, dy = SIDES[k]
        return pltpu.make_async_remote_copy(
            src_ref=side_part(k, agg_ref.at[0]), dst_ref=side_part(k, agg_side.at[k ^ 1]),
            send_sem=side_s.at[k], recv_sem=side_r.at[k ^ 1],
            device_id={"layer": lay + da, "tx": tx + dx, "ty": ty + dy}, device_id_type=MESH)

    def side_arrival(k):
        da, dx, dy = SIDES[k]
        return pltpu.make_async_remote_copy(
            src_ref=side_part(k ^ 1, agg_ref.at[0]), dst_ref=side_part(k ^ 1, agg_side.at[k]),
            send_sem=side_s.at[k], recv_sem=side_r.at[k],
            device_id={"layer": lay + da, "tx": tx + dx, "ty": ty + dy}, device_id_type=MESH)

    def field_each(step):
        for k, side in enumerate(SIDES):
            @pl.when(beside_layer(*side))
            def _(k=k):
                step(k)

    shunt = shunt_ref[0]
    diagonal = shunt + (4.0 + 2.0 * VIA_CONDUCTANCE)
    own_diag = 4.0 * COARSE_EDGE + restrict(shunt + 2.0 * VIA_CONDUCTANCE)
    coarse_out[ITERS] = flatten(own_diag)
    inverse = 1.0 / diagonal

    pl.semaphore_wait(barrier, everyone - 1)

    def slot_copy(k):
        return pltpu.make_async_remote_copy(
            src_ref=msg.at[lax.rem(me + k, tiles)], dst_ref=box.at[me],
            send_sem=msg_s, recv_sem=msg_r,
            device_id=tile_device(lax.rem(me + k, tiles)), device_id_type=MESH)

    def slot_all():
        return pltpu.make_async_remote_copy(
            src_ref=msg.at[pl.ds(0, tiles - 1)], dst_ref=box.at[pl.ds(0, tiles - 1)],
            send_sem=msg_s, recv_sem=msg_r,
            device_id=tile_device(lax.rem(me + 1, tiles)), device_id_type=MESH)

    each(tiles, lambda k: slot_copy(k).start())
    box[me] = msg[me]
    field_each(lambda k: side_copy(k).start())
    coarse_each(lambda k: coarse_copy(ITERS, k).start())

    slot_all().wait_recv()

    def scatter(first):
        lefts, rights = [], []
        for k in range(8):
            amount = box[first + k, 0:1, :]
            node = box[first + k, 1:2, :].astype(jnp.int32)
            row = node // breadth
            col = node % breadth
            hot = iota((height, breadth), 0) == row
            parts = []
            for _ in range(3):
                rounded = amount.astype(jnp.bfloat16).astype(jnp.float32)
                parts.append(jnp.where(hot, rounded, 0.0).astype(jnp.bfloat16))
                amount = amount - rounded
            lefts.append(jnp.concatenate(parts, axis=0))
            hot = iota((breadth, breadth), 0) == col
            rights.append(jnp.where(hot, 1.0, 0.0).astype(jnp.bfloat16))
        full = lax.dot_general(
            jnp.concatenate(lefts, axis=1), jnp.concatenate(rights, axis=1),
            (((1,), (1,)), ((), ())), preferred_element_type=jnp.float32)
        return full[:height] + full[height:2 * height] + full[2 * height:]

    if tiles == 8:
        sources = scatter(0)
    else:
        sources = lax.fori_loop(
            0, tiles // 8, lambda g, total: total + scatter(8 * g),
            jnp.zeros((height, breadth), jnp.float32))

    big = (height, breadth)
    big_lane = iota(big, 1)
    big_row = iota(big, 0)
    power = sources
    powers, smooths = [sources], []
    for turn in range(ITERS):
        local = power * inverse
        field_out[turn] = local
        field_each(lambda k: field_copy(turn, k).start())
        own = restrict(power)
        coarse_out[turn] = flatten(own)
        coarse_each(lambda k: coarse_copy(turn, k).start())
        if turn == 0:
            slot_all().wait_send()
            coarse_each(lambda k: coarse_copy(ITERS, k).wait_send())
            coarse_each(lambda k: coarse_arrival(ITERS, k).wait_recv())
            field_each(lambda k: side_copy(k).wait_send())
            field_each(lambda k: side_arrival(k).wait_recv())
            coarse_diag = coarse_blocks(ITERS, own_diag)
            coarse_inverse = [
                jnp.where(d > 0.0, RELAXATION / jnp.maximum(d, 1.0), 0.0) for d in coarse_diag]
        else:
            field_each(lambda k: field_copy(turn - 1, k).wait_send())
            coarse_each(lambda k: coarse_copy(turn - 1, k).wait_send())
        field_each(lambda k: field_arrival(turn, k).wait_recv())
        coarse_each(lambda k: coarse_arrival(turn, k).wait_recv())
        same, other = [
            sweeps(*x) for x in zip(coarse_blocks(turn, own), coarse_diag, coarse_inverse)]

        def table(block, row, g):
            part = block[CGX * row:CGX * (row + 1)]
            part = jnp.take_along_axis(
                part, CGY * g + lane % CGY, axis=1, mode="promise_in_bounds")
            return flatten(part)

        def spread(row, labels):
            return jnp.concatenate(
                [pick(row, labels[8 * i:8 * i + 8]) for i in range(labels.shape[0] // 8)], axis=0)

        smooth = local + spread(table(same, reach, 2), agg)
        below = field_in[turn, 0] + spread(table(other, 1, 1), agg_side[0])
        above = field_in[turn, 1] + spread(table(other, 1, 4), agg_side[1])
        west = field_in[turn, 4] + spread(table(same, reach, 1), agg_side[4])
        east = field_in[turn, 5] + spread(table(same, reach, 3), agg_side[5])
        north = field_in[turn, 2, height - 8:height, :] + pick(
            table(same, reach - 1, 2), agg_side[2, height - 8:height, :])
        south = field_in[turn, 3, 0:8, :] + pick(
            table(same, reach + 1, 2), agg_side[3, 0:8, :])
        north = jnp.where(big_row == 0, north[7:8, :], pltpu.roll(smooth, 1, 0))
        south = jnp.where(big_row == height - 1, south[0:1, :], pltpu.roll(smooth, height - 1, 0))
        west = pltpu.roll(jnp.where(big_lane == breadth - 1, west, smooth), 1, 1)
        east = pltpu.roll(jnp.where(big_lane == 0, east, smooth), breadth - 1, 1)
        image = (diagonal * smooth - (north + south + west + east)
                 - VIA_CONDUCTANCE * (below + above))
        power = image - SHIFT * power
        powers.append(power)
        smooths.append(smooth)

    sums = [
        jnp.sum(powers[(k + 1) // 2] * smooths[k // 2], axis=0, keepdims=True)
        for k in range(2 * ITERS)
    ]
    sums.append(jnp.zeros((8 - 2 * ITERS, breadth), jnp.float32))
    sums = jnp.sum(jnp.concatenate(sums, axis=0), axis=1, keepdims=True)
    spot = iota((8, breadth), 0) == lane
    part_out[...] = jnp.sum(jnp.where(spot, sums, 0.0), axis=0, keepdims=True)

    def part_copy(k):
        return pltpu.make_async_remote_copy(
            src_ref=part_out, dst_ref=part_in.at[place], send_sem=part_s, recv_sem=part_r,
            device_id=any_device(lax.rem(place + k, everyone)), device_id_type=MESH)

    def part_all():
        rows = part_in.at[pl.ds(0, everyone - 1)]
        return pltpu.make_async_remote_copy(
            src_ref=rows, dst_ref=rows, send_sem=part_s, recv_sem=part_r,
            device_id=any_device(lax.rem(place + 1, everyone)), device_id_type=MESH)

    each(everyone, lambda k: part_copy(k).start())
    part_in[place] = part_out[...]
    coarse_each(lambda k: coarse_copy(ITERS - 1, k).wait_send())
    field_each(lambda k: field_copy(ITERS - 1, k).wait_send())
    part_all().wait_recv()
    sums = jnp.sum(part_in[...], axis=0)
    sums = jnp.sum(jnp.where(spot, sums, 0.0), axis=1, keepdims=True)
    moments = [sums[k:k + 1, :] for k in range(2 * ITERS)]
    energies = [moments[k + 1] + SHIFT * moments[k] for k in range(2 * ITERS - 1)]

    res, way, volt = [1.0], [1.0], []
    curv = moments[0]
    for turn in range(ITERS):
        step = curv / quadratic(energies, way)
        volt = [(volt[i] if i < len(volt) else 0.0) + step * way[i] for i in range(turn + 1)]
        image = [0.0] * (turn + 2)
        for i in range(turn + 1):
            image[i + 1] = image[i + 1] + way[i]
            image[i] = image[i] + SHIFT * way[i]
        res = [(res[i] if i < len(res) else 0.0) - step * image[i] for i in range(turn + 2)]
        if turn + 1 < ITERS:
            newer = quadratic(moments, res)
            ratio = newer / curv
            way = [res[i] + (ratio * way[i] if i < len(way) else 0.0) for i in range(turn + 2)]
            curv = newer
    voltage = volt[0] * smooths[0]
    residual = res[0] * powers[0]
    for i in range(1, ITERS):
        voltage = voltage + volt[i] * smooths[i]
    for i in range(1, ITERS + 1):
        residual = residual + res[i] * powers[i]
    result_ref[0] = voltage
    result_ref[1] = residual
    part_all().wait_send()


def solution(mesh):
    layers, n_tx, n_ty = mesh.shape["layer"], mesh.shape["tx"], mesh.shape["ty"]
    tiles = n_tx * n_ty

    def body(shunt, agg, current, node, count):
        height, breadth = shunt.shape[1], shunt.shape[2]
        near = len(coarse_places(n_tx, n_ty))
        f32 = jnp.float32
        dma = pltpu.SemaphoreType.DMA
        vmem = pl.BlockSpec(memory_space=pltpu.VMEM)
        out = pl.pallas_call(
            functools.partial(kernel, (layers, n_tx, n_ty)),
            out_shape=jax.ShapeDtypeStruct((2,) + shunt.shape[1:], f32),
            in_specs=[pl.BlockSpec(memory_space=pltpu.HBM)] * 5,
            out_specs=vmem,
            scratch_shapes=[
                *(pltpu.VMEM(x.shape, x.dtype) for x in (shunt, agg, current, node, count)),
                dma((5,)),
                pltpu.VMEM((tiles, 2, current.shape[4]), f32),
                pltpu.VMEM((tiles, 2, current.shape[4]), f32),
                pltpu.VMEM((6, height, breadth), jnp.int32),
                pltpu.VMEM((height, CGX, breadth), f32),
                pltpu.VMEM((CGY * height // 2, 2 * breadth), jnp.bfloat16),
                pltpu.VMEM((ITERS + 1, 1, breadth), f32),
                pltpu.VMEM((ITERS + 1, near, 1, breadth), f32),
                pltpu.VMEM((ITERS, height, breadth), f32),
                pltpu.VMEM((ITERS, 6, height, breadth), f32),
                pltpu.VMEM((1, breadth), f32),
                pltpu.VMEM((layers * tiles, 1, breadth), f32),
                dma, dma,
                dma((6,)), dma((6,)),
                dma((ITERS + 1, near)), dma((ITERS + 1, near)),
                dma((ITERS, 6)), dma((ITERS, 6)),
                dma, dma,
            ],
            compiler_params=pltpu.CompilerParams(
                collective_id=0, has_side_effects=True, vmem_limit_bytes=60 * 1024 * 1024),
        )(shunt, agg, current, node, count)
        return out[0:1], out[1:2]

    in_specs = (
        P("layer", "tx", "ty"),
        P("layer", "tx", "ty"),
        P("layer", "tx", "ty", None, None),
        P("layer", "tx", "ty", None, None),
        P("layer", "tx", "ty", None),
    )
    out_specs = (P("layer", "tx", "ty"), P("layer", "tx", "ty"))

    def run(*args):
        voltage, residual = jax.shard_map(
            body, mesh=mesh, in_specs=in_specs, out_specs=out_specs, check_vma=False)(*args)
        return voltage, residual

    return run
```
